32 devices in a mesh: grp: 2 (over y), tp: 4 (over z), dp: 4 (over x, core).
Axes of the slice: x: 2, y: 2, z: 4, core: 2. Of those that a mesh axis runs over, the one named last changes fastest.
Arguments:
- layer_inputs: bfloat16 [16384, 8192], P(('grp', 'dp'), 'tp'), parts along dimension 0, may hold values from -6 to 6
- out_grads: bfloat16 [16384, 28672], P(('grp', 'dp'), 'tp'), parts along dimension 0, may hold values from -6 to 6
- doc_ids: int32 [8, 2048], P(('grp', 'dp')), parts along dimension 0, may hold values from 0 to 15, never falling along the last dimension, each value on 1 to 256 neighbouring positions
- proj_in: bfloat16 [8192, 64], P('tp'), may hold values from -0.0625 to 0.0625
- proj_out: bfloat16 [28672, 64], P('tp'), may hold values from -0.03125 to 0.03125
- query_feats: bfloat16 [4096, 1024], P('tp'), may hold values from -0.0078125 to 0.0078125
Outputs:
- scores: float32 [128, 1024], P(('grp', 'dp'), 'tp'), parts along dimension 0
The draws below stay inside these ranges and needn't reach their ends.
There are 2 independent parts, one for each index of `grp`. The reference program is written for one: setup_inputs(seed, part) draws one part's arguments, and reference() takes and returns one part's arrays. A program takes and returns all parts, laid end to end along the dimension named above; an argument that names none is the same for every part. Nothing has to cross between parts.
Inputs may be any that keep to these rules, and one draw needn't show every extreme that they name: `doc_ids`: each row is non-decreasing; every label appears, on at most 256 tokens.
All inputs are finite; a program needn't handle non-finite values.
Results may differ from the reference program's by a relative error of at most 0.0049.
Values may be sent and summed in bfloat16 or wider, within the bound.
A program may use at most 128 MiB of HBM per device.

```python
import math
import jax
import jax.numpy as jnp
import numpy as np

D = 8192
FF = 28672
PI = 64
PO = 64
QUERIES = 1024
TOK_DEV = 2048
DOCS_DEV = 16
FEATURES = 4096
GROUPS = 4
TOKENS = 8192


def steps_of(stream_key, dims, pieces, smallest, largest):
    level, own = 1.0, jax.random.fold_in(stream_key, 6)
    for position, parts in pieces:
        draws = jnp.exp(jax.random.uniform(jax.random.fold_in(own, position), (parts,), jnp.float32, smallest / len(pieces), largest / len(pieces)))
        level = level * jnp.repeat(draws, dims[position] // parts).reshape([-1 if axis == position else 1 for axis in range(len(dims))])
    return level


def length_profile(number_of, total, bound, lean):
    weights = [(1 << 20) // math.isqrt(standing ** lean) + 1 for standing in range(2, number_of + 1)]
    rest, given = total - bound - (number_of - 1), [1] * (number_of - 1)
    while rest > 0:
        free = [i for i in range(number_of - 1) if given[i] < bound]
        mass, remaining = sum([weights[i] for i in free]), rest
        for i in free:
            addition = min(bound - given[i], max(1, remaining * weights[i] // mass), rest)
            given[i] = given[i] + addition
            rest = rest - addition
    return np.array([bound] + given)


def uneven(key, number_of, total, reach, skew):
    if number_of == 2:
        one = jax.random.randint(key, (), max(1, total - reach), min(reach, total - 1) + 1)
        return jnp.stack([one, total - one])
    sizes = jnp.asarray(length_profile(number_of, total, reach, skew), jnp.int32)
    twos = (number_of - 1) // 2
    giver, sink = sizes[1:1 + 2 * twos:2], sizes[2:2 + 2 * twos:2]
    room = jnp.minimum(giver - 1, reach - sink)
    passed = jax.random.randint(jax.random.fold_in(key, 1), (twos,), 0, 1 << 20) % (room + 1)
    sizes = sizes.at[1:1 + 2 * twos:2].set(giver - passed).at[2:2 + 2 * twos:2].set(sink + passed)
    return sizes[jax.random.permutation(jax.random.fold_in(key, 2), number_of)]


def bell_draw(key, dims, deviation, limit, pieces=(), held_as=jnp.bfloat16):
    factor_of = steps_of(key, dims, pieces, -0.22, 0.18) if pieces else 1.0
    drawn = jax.random.normal(key, dims, jnp.float32) * deviation * factor_of
    return jnp.minimum(jnp.maximum(drawn, -limit), limit).astype(held_as)


def setup_inputs(seed: int = 0, part: int = 0) -> dict:
    key_of = jax.random.split(jax.random.key(seed), 7)
    own_keys = jax.random.split(jax.random.fold_in(key_of[6], part), 7)
    return {
        "layer_inputs": bell_draw(own_keys[0], (TOKENS, D), 1.0, 6.0, ((0, 4), (1, 4))),
        "out_grads": bell_draw(own_keys[1], (TOKENS, FF), 1.0, 6.0, ((0, 4), (1, 4))),
        "doc_ids": jax.vmap(lambda own: jnp.searchsorted(jnp.cumsum(uneven(own, DOCS_DEV, TOK_DEV, TOK_DEV // 8, 1)), jnp.arange(TOK_DEV), side="right"))(jax.random.split(own_keys[2], GROUPS)).reshape((GROUPS, TOK_DEV)).astype(jnp.int32),
        "proj_in": bell_draw(key_of[3], (D, PI), D ** -0.5, 0.0625, ((0, 4),)),
        "proj_out": bell_draw(key_of[4], (FF, PO), FF ** -0.5, 0.03125, ((0, 4),)),
        "query_feats": bell_draw(key_of[5], (FEATURES, QUERIES), (FEATURES * 128) ** -0.5, 0.0078125, ((0, 4),)),
    }


def reference(layer_inputs, out_grads, doc_ids, proj_in, proj_out, query_feats):
    in_proj = jnp.dot(layer_inputs, proj_in, preferred_element_type=jnp.float32).astype(jnp.bfloat16)
    out_proj = jnp.dot(out_grads, proj_out, preferred_element_type=jnp.float32).astype(jnp.bfloat16)
    groups = doc_ids.shape[0]
    tok_rows = doc_ids.shape[1]
    labels = jnp.arange(DOCS_DEV, dtype=jnp.int32)
    onehot = (doc_ids[:, :, None] == labels[None, None, :]).astype(jnp.float32)
    left = in_proj.astype(jnp.float32).reshape(groups, tok_rows, PI)
    right = out_proj.astype(jnp.float32).reshape(groups, tok_rows, PO)
    feats = jnp.einsum("nte,nti,ntj->neji", onehot, left, right)
    doc_feats = feats.reshape(groups * DOCS_DEV, PO * PI).astype(jnp.bfloat16)
    return jnp.dot(doc_feats, query_feats, preferred_element_type=jnp.float32)
```

```python
import functools

import jax
import jax.numpy as jnp
from jax import lax
from jax.experimental import pallas as pl
from jax.experimental.pallas import tpu as pltpu
from jax.sharding import PartitionSpec as P

PI = 64
PO = 64
DOCS_DEV = 16
MESH = pl.DeviceIdType.MESH
BLOCK = 128


def kernel(
    n, block,
    x_hbm, g_hbm, ids_hbm, wi_hbm, wo_hbm, q_hbm, o_ref,
    x, g, ids, wi, wo, q, part, own, part_in, out_t, feat, feat_in, score, score_in,
    load_sem, const_sem, part_send, part_recv, feat_send, feat_recv, score_send, score_recv,
):
    tokens = x.shape[0]
    share = tokens // n
    chunks = share // block
    far = (n - 1) * chunks
    cols = PO // n
    me = lax.axis_index("tp")

    def peer(k):
        return lax.rem(me + 1 + k, n)

    barrier = pltpu.get_barrier_semaphore()
    for k in range(n - 1):
        pl.semaphore_signal(barrier, inc=1, device_id={"tp": peer(k)}, device_id_type=MESH)

    def rows(step):
        k, c = step // chunks, step % chunks
        return pl.ds(pl.multiple_of(peer(k) * share + c * block, block), block)

    def load_x(step):
        at = rows(step)
        return pltpu.make_async_copy(x_hbm.at[at], x.at[at], load_sem.at[0, step])

    def load_g(step):
        at = rows(step)
        return pltpu.make_async_copy(g_hbm.at[at], g.at[at], load_sem.at[1, step])

    load_wi = pltpu.make_async_copy(wi_hbm, wi, const_sem.at[0])
    load_wo = pltpu.make_async_copy(wo_hbm, wo, const_sem.at[1])
    load_q = pltpu.make_async_copy(q_hbm, q, const_sem.at[2])
    load_ids = pltpu.make_async_copy(
        ids_hbm.at[:, pl.ds(pl.multiple_of(me * share, share), share)], ids, const_sem.at[3]
    )

    load_wi.start()
    load_x(0).start()
    load_wo.start()
    load_g(0).start()

    def start_loads(step, carry):
        load_x(step).start()
        load_g(step).start()
        return carry

    lax.fori_loop(1, n * chunks, start_loads, 0)
    load_ids.start()
    load_q.start()

    def project(step):
        at = rows(step)
        load_x(step).wait()
        in_part = jnp.dot(x[at, :], wi[...], preferred_element_type=jnp.float32)
        load_g(step).wait()
        out_part = jnp.dot(g[at, :], wo[...], preferred_element_type=jnp.float32)
        return jnp.concatenate([in_part, out_part], axis=1)

    def send_part(step):
        k, c = step // chunks, step % chunks
        here = pl.ds(pl.multiple_of(c * block, block), block)
        return pltpu.make_async_remote_copy(
            src_ref=part.at[k, here],
            dst_ref=part_in.at[k, here],
            send_sem=part_send.at[step],
            recv_sem=part_recv.at[step],
            device_id={"tp": peer(k)},
            device_id_type=MESH,
        )

    load_wi.wait()
    load_wo.wait()
    pl.semaphore_wait(barrier, n - 1)

    def far_step(step, carry):
        k, c = step // chunks, step % chunks
        here = pl.ds(pl.multiple_of(c * block, block), block)
        part[k, here, :] = project(step).astype(jnp.bfloat16)
        send_part(step).start()
        return carry

    lax.fori_loop(0, far, far_step, 0)

    def own_step(c, carry):
        here = pl.ds(pl.multiple_of(c * block, block), block)
        own[here, :] = project(far + c)
        return carry

    lax.fori_loop(0, chunks, own_step, 0)

    def drain(step, carry):
        copy = send_part(step)
        copy.wait_send()
        copy.wait_recv()
        return carry

    lax.fori_loop(0, far, drain, 0)

    total = own[...]
    for k in range(n - 1):
        total = total + part_in[k].astype(jnp.float32)
    both = total.astype(jnp.bfloat16).astype(jnp.float32)
    lane = lax.broadcasted_iota(jnp.int32, both.shape, 1)
    twice = jnp.where(lane < PI, both, pltpu.roll(both, PI, 1)).astype(jnp.bfloat16)
    flipped = both.T
    for d in range(n):
        out_t[d] = flipped[PI + d * cols:PI + (d + 1) * cols, :]

    load_ids.wait()
    docs = lax.broadcasted_iota(jnp.int32, (DOCS_DEV, share), 0)
    mask = ids[...] == docs

    def doc_features(d):
        mine = out_t[d]
        spread = jnp.concatenate(
            [jnp.where(mask, mine[j:j + 1, :], 0.0).astype(jnp.bfloat16) for j in range(cols)], axis=0
        )
        feats = jnp.dot(spread, twice, preferred_element_type=jnp.float32)
        half = lax.broadcasted_iota(jnp.int32, (DOCS_DEV, 2 * PI), 1) < PI
        return [
            jnp.where(
                half,
                feats[2 * jp * DOCS_DEV:(2 * jp + 1) * DOCS_DEV],
                feats[(2 * jp + 1) * DOCS_DEV:(2 * jp + 2) * DOCS_DEV],
            )
            for jp in range(cols // 2)
        ]

    def send_feat(k):
        return pltpu.make_async_remote_copy(
            src_ref=feat.at[k],
            dst_ref=feat_in.at[k],
            send_sem=feat_send.at[k],
            recv_sem=feat_recv.at[k],
            device_id={"tp": peer(k)},
            device_id_type=MESH,
        )

    for k in range(n - 1):
        for jp, rows_jp in enumerate(doc_features(peer(k))):
            feat[k, jp] = rows_jp.astype(jnp.bfloat16)
        send_feat(k).start()
    sums = doc_features(me)
    load_q.wait()
    for k in range(n - 1):
        send_feat(k).wait_recv()
        sums = [s + feat_in[k, jp].astype(jnp.float32) for jp, s in enumerate(sums)]
    left = jnp.concatenate([s.astype(jnp.bfloat16) for s in sums], axis=1)
    scores = jnp.dot(left, q[...], preferred_element_type=jnp.float32)
    width = scores.shape[1] // n
    for d in range(n):
        score[d] = scores[:, d * width:(d + 1) * width]

    def send_score(k):
        return pltpu.make_async_remote_copy(
            src_ref=score.at[peer(k)],
            dst_ref=score_in.at[k],
            send_sem=score_send.at[k],
            recv_sem=score_recv.at[k],
            device_id={"tp": peer(k)},
            device_id_type=MESH,
        )

    for k in range(n - 1):
        send_score(k).start()
    result = score[me]
    for k in range(n - 1):
        send_score(k).wait_recv()
        result = result + score_in[k]
    o_ref[...] = result
    for k in range(n - 1):
        send_feat(k).wait_send()
        send_score(k).wait_send()


def per_device(n, layer_inputs, out_grads, doc_ids, proj_in, proj_out, query_feats):
    tokens = layer_inputs.shape[0]
    share = tokens // n
    block = min(BLOCK, share)
    steps = tokens // block
    far = (n - 1) * (share // block)
    cols = PO // n
    queries = query_feats.shape[1]
    width = queries // n
    wide = PI + PO
    bf16, f32 = jnp.bfloat16, jnp.float32
    flops = 2 * tokens * (proj_in.size + proj_out.size)
    moved = 2 * (layer_inputs.size + out_grads.size + proj_in.size + proj_out.size + query_feats.size)
    return pl.pallas_call(
        functools.partial(kernel, n, block),
        out_shape=jax.ShapeDtypeStruct((DOCS_DEV, width), f32),
        in_specs=[pl.BlockSpec(memory_space=pl.ANY)] * 6,
        out_specs=pl.BlockSpec(memory_space=pltpu.VMEM),
        scratch_shapes=[
            pltpu.VMEM(layer_inputs.shape, bf16),
            pltpu.VMEM(out_grads.shape, bf16),
            pltpu.VMEM((1, share), jnp.int32),
            pltpu.VMEM(proj_in.shape, bf16),
            pltpu.VMEM(proj_out.shape, bf16),
            pltpu.VMEM(query_feats.shape, bf16),
            pltpu.VMEM((n - 1, share, wide), bf16),
            pltpu.VMEM((share, wide), f32),
            pltpu.VMEM((n - 1, share, wide), bf16),
            pltpu.VMEM((n, cols, share), f32),
            pltpu.VMEM((n - 1, cols // 2, DOCS_DEV, 2 * PI), bf16),
            pltpu.VMEM((n - 1, cols // 2, DOCS_DEV, 2 * PI), bf16),
            pltpu.VMEM((n, DOCS_DEV, width), f32),
            pltpu.VMEM((n - 1, DOCS_DEV, width), f32),
            pltpu.SemaphoreType.DMA((2, steps)),
            pltpu.SemaphoreType.DMA((4,)),
            pltpu.SemaphoreType.DMA((far,)),
            pltpu.SemaphoreType.DMA((far,)),
            pltpu.SemaphoreType.DMA((n - 1,)),
            pltpu.SemaphoreType.DMA((n - 1,)),
            pltpu.SemaphoreType.DMA((n - 1,)),
            pltpu.SemaphoreType.DMA((n - 1,)),
        ],
        compiler_params=pltpu.CompilerParams(
            collective_id=0, has_side_effects=True, vmem_limit_bytes=56 * 1024 * 1024
        ),
        cost_estimate=pl.CostEstimate(flops=flops, bytes_accessed=moved, transcendentals=0),
    )(layer_inputs, out_grads, doc_ids, proj_in, proj_out, query_feats)


def solution(mesh):
    return jax.shard_map(
        functools.partial(per_device, mesh.shape["tp"]),
        mesh=mesh,
        in_specs=(
            P(("grp", "dp"), "tp"),
            P(("grp", "dp"), "tp"),
            P(("grp", "dp"), None),
            P("tp", None),
            P("tp", None),
            P("tp", None),
        ),
        out_specs=P(("grp", "dp"), "tp"),
        check_vma=False,
    )
```

```python
import functools

import jax
import jax.numpy as jnp
from jax import lax
from jax.experimental import pallas as pl
from jax.experimental.pallas import tpu as pltpu
from jax.sharding import PartitionSpec as P

PI = 64
PO = 64
DOCS_DEV = 16
MESH = pl.DeviceIdType.MESH
CHUNK = 7168


def across(a, b):
    return lax.dot_general(a, b, (((1,), (1,)), ((), ())), preferred_element_type=jnp.float32)


def chunks_of(width):
    chunk = CHUNK if width % CHUNK == 0 else width
    return [pl.ds(i, chunk) for i in range(0, width, chunk)]


def kernel(
    n,
    x_hbm, g_hbm, ids_hbm, wi_hbm, wo_hbm, q_hbm, o_ref,
    x, g, ids, wi, wo, q, part, own, part_in, out_t, feat, feat_in, score, score_out, score_in,
    load_sem, const_sem, part_send, part_recv, feat_send, feat_recv, score_send, score_recv,
):
    share = x.shape[0] // n
    cols = PO // n
    half_way = n // 2
    me = lax.axis_index("tp")
    pieces = [(x_hbm, x, wi, at) for at in chunks_of(x.shape[1])]
    pieces += [(g_hbm, g, wo, at) for at in chunks_of(g.shape[1])]

    def peer(k):
        away = k + k // half_way + (1 - (k + n - 1) // n) * half_way
        return lax.rem(me + away, n)

    barrier = pltpu.get_barrier_semaphore()
    for k in range(n - 1):
        pl.semaphore_signal(barrier, inc=1, device_id={"tp": peer(k)}, device_id_type=MESH)

    def rows(k):
        return pl.ds(pl.multiple_of(peer(k) * share, share), share)

    def load(k, i):
        source, target, _, at = pieces[i]
        return pltpu.make_async_copy(source.at[rows(k), at], target.at[rows(k), at], load_sem.at[i, k])

    load_wi = pltpu.make_async_copy(wi_hbm, wi, const_sem.at[0])
    load_wo = pltpu.make_async_copy(wo_hbm, wo, const_sem.at[1])
    load_q = pltpu.make_async_copy(q_hbm, q, const_sem.at[2])
    load_ids = pltpu.make_async_copy(
        ids_hbm.at[:, pl.ds(pl.multiple_of(me * share, share), share)], ids, const_sem.at[3]
    )

    load_wi.start()
    load(0, 0).start()
    load_wo.start()
    for i in range(1, len(pieces)):
        load(0, i).start()

    def start_loads(k, carry):
        for i in range(len(pieces)):
            load(k, i).start()
        return carry

    lax.fori_loop(1, n, start_loads, 0)
    load_ids.start()
    load_q.start()

    def send_part(k, side):
        return pltpu.make_async_remote_copy(
            src_ref=part.at[k, side],
            dst_ref=part_in.at[k, side],
            send_sem=part_send.at[side, k],
            recv_sem=part_recv.at[side, k],
            device_id={"tp": peer(k)},
            device_id_type=MESH,
        )

    load_wi.wait()
    load_wo.wait()
    pl.semaphore_wait(barrier, n - 1)

    def project(k, carry):
        for side, weight in enumerate((wi, wo)):
            done = 0.0
            for i, (_, data, held, at) in enumerate(pieces):
                if held is weight:
                    load(k, i).wait()
                    done = done + across(weight[:, at], data[rows(k), at])
            own[side] = done

            @pl.when(k < n - 1)
            def _():
                part[k, side] = done.astype(jnp.bfloat16)
                send_part(k, side).start()

        return carry

    lax.fori_loop(0, n, project, 0)

    total = own[...]
    for k in range(n - 1):
        send_part(k, 0).wait_recv()
        send_part(k, 1).wait_recv()
        total = total + part_in[k].astype(jnp.float32)
    high = total[0].astype(jnp.bfloat16)
    low = (total[0] - high.astype(jnp.float32)).astype(jnp.bfloat16)
    twice = jnp.concatenate([high, high, low, low], axis=0)
    flipped = total[1].astype(jnp.bfloat16).astype(jnp.float32)
    for d in range(n):
        out_t[d] = flipped[d * cols:(d + 1) * cols, :]

    load_ids.wait()
    docs = lax.broadcasted_iota(jnp.int32, (DOCS_DEV, share), 0)
    mask = ids[...] == docs

    def doc_features(d):
        mine = out_t[d]
        spread = jnp.concatenate(
            [jnp.where(mask, mine[j:j + 1, :], 0.0).astype(jnp.bfloat16) for j in range(cols)], axis=0
        )
        feats = across(spread, twice)
        feats = feats[:, :2 * PI] + feats[:, 2 * PI:]
        half = lax.broadcasted_iota(jnp.int32, (DOCS_DEV, 2 * PI), 1) < PI
        return [
            jnp.where(
                half,
                feats[2 * jp * DOCS_DEV:(2 * jp + 1) * DOCS_DEV],
                feats[(2 * jp + 1) * DOCS_DEV:(2 * jp + 2) * DOCS_DEV],
            )
            for jp in range(cols // 2)
        ]

    def send_feat(k):
        return pltpu.make_async_remote_copy(
            src_ref=feat.at[k],
            dst_ref=feat_in.at[k],
            send_sem=feat_send.at[k],
            recv_sem=feat_recv.at[k],
            device_id={"tp": peer(k)},
            device_id_type=MESH,
        )

    for k in range(n - 1):
        for jp, rows_jp in enumerate(doc_features(peer(k))):
            feat[k, jp] = rows_jp.astype(jnp.bfloat16)
        send_feat(k).start()
    sums = doc_features(me)
    load_q.wait()
    for k in range(n - 1):
        send_feat(k).wait_recv()
        sums = [s + feat_in[k, jp].astype(jnp.float32) for jp, s in enumerate(sums)]
    left = jnp.concatenate(sums, axis=1)
    high = left.astype(jnp.bfloat16)
    low = (left - high.astype(jnp.float32)).astype(jnp.bfloat16)
    scores = jnp.dot(jnp.concatenate([high, low], axis=0), q[...], preferred_element_type=jnp.float32)
    scores = scores[:DOCS_DEV] + scores[DOCS_DEV:]
    width = scores.shape[1] // n
    for d in range(n):
        score[d] = scores[:, d * width:(d + 1) * width]
        score_out[d] = score[d].astype(jnp.bfloat16)

    def send_score(k):
        return pltpu.make_async_remote_copy(
            src_ref=score_out.at[peer(k)],
            dst_ref=score_in.at[k],
            send_sem=score_send.at[k],
            recv_sem=score_recv.at[k],
            device_id={"tp": peer(k)},
            device_id_type=MESH,
        )

    for k in range(n - 1):
        send_score(k).start()
    result = score[me]
    for k in range(n - 1):
        send_score(k).wait_recv()
        result = result + score_in[k].astype(jnp.float32)
    o_ref[...] = result
    for k in range(n - 1):
        send_part(k, 0).wait_send()
        send_part(k, 1).wait_send()
        send_feat(k).wait_send()
        send_score(k).wait_send()


def per_device(n, layer_inputs, out_grads, doc_ids, proj_in, proj_out, query_feats):
    tokens = layer_inputs.shape[0]
    share = tokens // n
    loads = len(chunks_of(layer_inputs.shape[1])) + len(chunks_of(out_grads.shape[1]))
    cols = PO // n
    queries = query_feats.shape[1]
    width = queries // n
    bf16, f32 = jnp.bfloat16, jnp.float32
    flops = 2 * tokens * (proj_in.size + proj_out.size)
    moved = 2 * (layer_inputs.size + out_grads.size + proj_in.size + proj_out.size + query_feats.size)
    return pl.pallas_call(
        functools.partial(kernel, n),
        out_shape=jax.ShapeDtypeStruct((DOCS_DEV, width), f32),
        in_specs=[pl.BlockSpec(memory_space=pl.ANY)] * 6,
        out_specs=pl.BlockSpec(memory_space=pltpu.VMEM),
        scratch_shapes=[
            pltpu.VMEM(layer_inputs.shape, bf16),
            pltpu.VMEM(out_grads.shape, bf16),
            pltpu.VMEM((1, share), jnp.int32),
            pltpu.VMEM(proj_in.shape[::-1], bf16),
            pltpu.VMEM(proj_out.shape[::-1], bf16),
            pltpu.VMEM(query_feats.shape, bf16),
            pltpu.VMEM((n - 1, 2, PI, share), bf16),
            pltpu.VMEM((2, PI, share), f32),
            pltpu.VMEM((n - 1, 2, PI, share), bf16),
            pltpu.VMEM((n, cols, share), f32),
            pltpu.VMEM((n - 1, cols // 2, DOCS_DEV, 2 * PI), bf16),
            pltpu.VMEM((n - 1, cols // 2, DOCS_DEV, 2 * PI), bf16),
            pltpu.VMEM((n, DOCS_DEV, width), f32),
            pltpu.VMEM((n, DOCS_DEV, width), bf16),
            pltpu.VMEM((n - 1, DOCS_DEV, width), bf16),
            pltpu.SemaphoreType.DMA((loads, n)),
            pltpu.SemaphoreType.DMA((4,)),
            pltpu.SemaphoreType.DMA((2, n - 1)),
            pltpu.SemaphoreType.DMA((2, n - 1)),
            pltpu.SemaphoreType.DMA((n - 1,)),
            pltpu.SemaphoreType.DMA((n - 1,)),
            pltpu.SemaphoreType.DMA((n - 1,)),
            pltpu.SemaphoreType.DMA((n - 1,)),
        ],
        compiler_params=pltpu.CompilerParams(
            collective_id=0, has_side_effects=True, vmem_limit_bytes=56 * 1024 * 1024
        ),
        cost_estimate=pl.CostEstimate(flops=flops, bytes_accessed=moved, transcendentals=0),
    )(layer_inputs, out_grads, doc_ids, proj_in.T, proj_out.T, query_feats)


def solution(mesh):
    return jax.shard_map(
        functools.partial(per_device, mesh.shape["tp"]),
        mesh=mesh,
        in_specs=(
            P(("grp", "dp"), "tp"),
            P(("grp", "dp"), "tp"),
            P(("grp", "dp"), None),
            P("tp", None),
            P("tp", None),
            P("tp", None),
        ),
        out_specs=P(("grp", "dp"), "tp"),
        check_vma=False,
    )
```

```python
import functools

import jax
import jax.numpy as jnp
from jax import lax
from jax.experimental import pallas as pl
from jax.experimental.pallas import tpu as pltpu
from jax.sharding import PartitionSpec as P

PI = 64
PO = 64
DOCS_DEV = 16
MESH = pl.DeviceIdType.MESH
CHUNK = 7168


def across(a, b):
    return lax.dot_general(a, b, (((1,), (1,)), ((), ())), preferred_element_type=jnp.float32)


def chunks_of(width):
    chunk = CHUNK if width % CHUNK == 0 else width
    return [pl.ds(i, chunk) for i in range(0, width, chunk)]


def kernel(
    n,
    x_hbm, g_hbm, ids_hbm, wi_hbm, wo_hbm, q_hbm, o_ref,
    x, g, ids, wi, wo, q, part, own, part_in, out_t, feat, feat_in, score, score_out, score_in,
    load_sem, const_sem, part_send, part_recv, feat_send, feat_recv, score_send, score_recv,
):
    share = x.shape[0] // n
    cols = PO // n
    half_way = n // 2
    me = lax.axis_index("tp")
    pieces = [(x_hbm, x, wi, at) for at in chunks_of(x.shape[1])]
    pieces += [(g_hbm, g, wo, at) for at in chunks_of(g.shape[1])]

    def peer(k):
        away = k + k // half_way + (1 - (k + n - 1) // n) * half_way
        return lax.rem(me + away, n)

    barrier = pltpu.get_barrier_semaphore()
    for k in range(n - 1):
        pl.semaphore_signal(barrier, inc=1, device_id={"tp": peer(k)}, device_id_type=MESH)

    def rows(k):
        return pl.ds(pl.multiple_of(peer(k) * share, share), share)

    def load(k, i):
        source, target, _, at = pieces[i]
        return pltpu.make_async_copy(source.at[rows(k), at], target.at[rows(k), at], load_sem.at[i, k])

    load_wi = pltpu.make_async_copy(wi_hbm, wi, const_sem.at[0])
    load_wo = pltpu.make_async_copy(wo_hbm, wo, const_sem.at[1])
    load_q = pltpu.make_async_copy(q_hbm, q, const_sem.at[2])
    load_ids = pltpu.make_async_copy(
        ids_hbm.at[:, pl.ds(pl.multiple_of(me * share, share), share)], ids, const_sem.at[3]
    )

    load_wi.start()
    load(0, 0).start()
    load_wo.start()
    for i in range(1, len(pieces)):
        load(0, i).start()

    def start_loads(k, carry):
        for i in range(len(pieces)):
            load(k, i).start()
        return carry

    lax.fori_loop(1, n, start_loads, 0)
    load_ids.start()
    load_q.start()

    def send_part(k, side):
        return pltpu.make_async_remote_copy(
            src_ref=part.at[k, side],
            dst_ref=part_in.at[k, side],
            send_sem=part_send.at[side, k],
            recv_sem=part_recv.at[side, k],
            device_id={"tp": peer(k)},
            device_id_type=MESH,
        )

    load_wi.wait()
    pl.semaphore_wait(barrier, n - 1)

    def project(k, carry):
        for side, weight in enumerate((wi, wo)):
            done = 0.0
            if side == 1:

                @pl.when(k == 0)
                def _():
                    load_wo.wait()

            for i, (_, data, held, at) in enumerate(pieces):
                if held is weight:
                    load(k, i).wait()
                    done = done + across(weight[:, at], data[rows(k), at])
            own[side] = done

            @pl.when(k < n - 1)
            def _():
                part[k, side] = done.astype(jnp.bfloat16)
                send_part(k, side).start()

        return carry

    lax.fori_loop(0, n, project, 0)

    total = own[...]
    for k in range(n - 1):
        send_part(k, 0).wait_recv()
        send_part(k, 1).wait_recv()
        total = total + part_in[k].astype(jnp.float32)
    high = total[0].astype(jnp.bfloat16)
    low = (total[0] - high.astype(jnp.float32)).astype(jnp.bfloat16)
    twice = jnp.concatenate([high, high, low, low], axis=0)
    flipped = total[1].astype(jnp.bfloat16).astype(jnp.float32)
    for d in range(n):
        out_t[d] = flipped[d * cols:(d + 1) * cols, :]

    load_ids.wait()
    docs = lax.broadcasted_iota(jnp.int32, (DOCS_DEV, share), 0)
    mask = ids[...] == docs

    def doc_features(d):
        mine = out_t[d]
        spread = jnp.concatenate(
            [jnp.where(mask, mine[j:j + 1, :], 0.0).astype(jnp.bfloat16) for j in range(cols)], axis=0
        )
        feats = across(spread, twice)
        feats = feats[:, :2 * PI] + feats[:, 2 * PI:]
        half = lax.broadcasted_iota(jnp.int32, (DOCS_DEV, 2 * PI), 1) < PI
        return [
            jnp.where(
                half,
                feats[2 * jp * DOCS_DEV:(2 * jp + 1) * DOCS_DEV],
                feats[(2 * jp + 1) * DOCS_DEV:(2 * jp + 2) * DOCS_DEV],
            )
            for jp in range(cols // 2)
        ]

    def send_feat(k):
        return pltpu.make_async_remote_copy(
            src_ref=feat.at[k],
            dst_ref=feat_in.at[k],
            send_sem=feat_send.at[k],
            recv_sem=feat_recv.at[k],
            device_id={"tp": peer(k)},
            device_id_type=MESH,
        )

    for k in range(n - 1):
        for jp, rows_jp in enumerate(doc_features(peer(k))):
            feat[k, jp] = rows_jp.astype(jnp.bfloat16)
        send_feat(k).start()
    sums = doc_features(me)
    load_q.wait()
    for k in range(n - 1):
        send_feat(k).wait_recv()
        sums = [s + feat_in[k, jp].astype(jnp.float32) for jp, s in enumerate(sums)]
    left = jnp.concatenate(sums, axis=1)
    high = left.astype(jnp.bfloat16)
    low = (left - high.astype(jnp.float32)).astype(jnp.bfloat16)
    scores = jnp.dot(jnp.concatenate([high, low], axis=0), q[...], preferred_element_type=jnp.float32)
    scores = scores[:DOCS_DEV] + scores[DOCS_DEV:]
    width = scores.shape[1] // n
    for d in range(n):
        score[d] = scores[:, d * width:(d + 1) * width]
        score_out[d] = score[d].astype(jnp.bfloat16)

    def send_score(k):
        return pltpu.make_async_remote_copy(
            src_ref=score_out.at[peer(k)],
            dst_ref=score_in.at[k],
            send_sem=score_send.at[k],
            recv_sem=score_recv.at[k],
            device_id={"tp": peer(k)},
            device_id_type=MESH,
        )

    for k in range(n - 1):
        send_score(k).start()
    result = score[me]
    for k in range(n - 1):
        send_score(k).wait_recv()
        result = result + score_in[k].astype(jnp.float32)
    o_ref[...] = result
    for k in range(n - 1):
        send_part(k, 0).wait_send()
        send_part(k, 1).wait_send()
        send_feat(k).wait_send()
        send_score(k).wait_send()


def per_device(n, layer_inputs, out_grads, doc_ids, proj_in, proj_out, query_feats):
    tokens = layer_inputs.shape[0]
    share = tokens // n
    loads = len(chunks_of(layer_inputs.shape[1])) + len(chunks_of(out_grads.shape[1]))
    cols = PO // n
    queries = query_feats.shape[1]
    width = queries // n
    bf16, f32 = jnp.bfloat16, jnp.float32
    flops = 2 * tokens * (proj_in.size + proj_out.size)
    moved = 2 * (layer_inputs.size + out_grads.size + proj_in.size + proj_out.size + query_feats.size)
    return pl.pallas_call(
        functools.partial(kernel, n),
        out_shape=jax.ShapeDtypeStruct((DOCS_DEV, width), f32),
        in_specs=[pl.BlockSpec(memory_space=pl.ANY)] * 6,
        out_specs=pl.BlockSpec(memory_space=pltpu.VMEM),
        scratch_shapes=[
            pltpu.VMEM(layer_inputs.shape, bf16),
            pltpu.VMEM(out_grads.shape, bf16),
            pltpu.VMEM((1, share), jnp.int32),
            pltpu.VMEM(proj_in.shape[::-1], bf16),
            pltpu.VMEM(proj_out.shape[::-1], bf16),
            pltpu.VMEM(query_feats.shape, bf16),
            pltpu.VMEM((n - 1, 2, PI, share), bf16),
            pltpu.VMEM((2, PI, share), f32),
            pltpu.VMEM((n - 1, 2, PI, share), bf16),
            pltpu.VMEM((n, cols, share), f32),
            pltpu.VMEM((n - 1, cols // 2, DOCS_DEV, 2 * PI), bf16),
            pltpu.VMEM((n - 1, cols // 2, DOCS_DEV, 2 * PI), bf16),
            pltpu.VMEM((n, DOCS_DEV, width), f32),
            pltpu.VMEM((n, DOCS_DEV, width), bf16),
            pltpu.VMEM((n - 1, DOCS_DEV, width), bf16),
            pltpu.SemaphoreType.DMA((loads, n)),
            pltpu.SemaphoreType.DMA((4,)),
            pltpu.SemaphoreType.DMA((2, n - 1)),
            pltpu.SemaphoreType.DMA((2, n - 1)),
            pltpu.SemaphoreType.DMA((n - 1,)),
            pltpu.SemaphoreType.DMA((n - 1,)),
            pltpu.SemaphoreType.DMA((n - 1,)),
            pltpu.SemaphoreType.DMA((n - 1,)),
        ],
        compiler_params=pltpu.CompilerParams(
            collective_id=0, has_side_effects=True, vmem_limit_bytes=56 * 1024 * 1024
        ),
        cost_estimate=pl.CostEstimate(flops=flops, bytes_accessed=moved, transcendentals=0),
    )(layer_inputs, out_grads, doc_ids, proj_in.T, proj_out.T, query_feats)


def solution(mesh):
    return jax.shard_map(
        functools.partial(per_device, mesh.shape["tp"]),
        mesh=mesh,
        in_specs=(
            P(("grp", "dp"), "tp"),
            P(("grp", "dp"), "tp"),
            P(("grp", "dp"), None),
            P("tp", None),
            P("tp", None),
            P("tp", None),
        ),
        out_specs=P(("grp", "dp"), "tp"),
        check_vma=False,
    )
```
